32 devices in a mesh: blk: 16 (over z, x, core), rep: 2 (over y).
Axes of the slice: x: 2, y: 2, z: 4, core: 2. Of those that a mesh axis runs over, the one named last changes fastest.
Arguments:
- image_emb: bfloat16 [16384, 1152], P(('blk', 'rep')), may hold values from -0.19921875 to 0.19921875
- text_emb: bfloat16 [16384, 1152], P(('blk', 'rep')), may hold values from -0.19921875 to 0.19921875
- log_temp: float32 [], replicated, may hold values from 1 to 2
- bias: float32 [], replicated, may hold values from -2 to 0
Outputs:
- row_loss: float32 [16384], P(('blk', 'rep'))
- grad_image: float32 [16384, 1152], P(('blk', 'rep'))
- grad_text: float32 [16384, 1152], P(('blk', 'rep'))
The draws below stay inside these ranges and needn't reach their ends.
All inputs are finite; a program needn't handle non-finite values.
Results may differ from the reference program's by a relative error of at most 0.0042.
Values may be sent and summed in bfloat16 or wider, within the bound.
A program may use at most 64 MiB of HBM per device.

```python
import jax
import jax.numpy as jnp
from jax import lax

D = 1152
ROWS = 512
STEPS = 4
TOKENS = 16384


def levels(key, shape, cuts, smallest, high):
    def one(dim, parts):
        draws = jax.random.uniform(jax.random.fold_in(jax.random.fold_in(key, 6), dim), (parts,), jnp.float32, smallest / len(cuts), high / len(cuts))
        return jnp.repeat(jnp.exp(draws), shape[dim] // parts).reshape((-1,) + (1,) * (len(shape) - dim - 1))

    loudness = one(*cuts[0])
    for cut in cuts[1:]:
        loudness = loudness * one(*cut)
    return loudness


def centred(own_key, shape, scale, reach, cuts=(), kind=jnp.bfloat16):
    values = scale * jax.random.normal(own_key, shape, jnp.float32)
    if cuts:
        values = values * levels(own_key, shape, cuts, -0.22, 0.18)
    return jnp.clip(values, -reach, reach).astype(kind)


def setup_inputs(seed: int = 0) -> dict:
    key_list = jax.random.split(jax.random.key(seed), 5)
    image_emb = centred(key_list[0], (TOKENS, D), 0.03, 0.19921875, ((0, 32),))
    text_emb = centred(key_list[1], (TOKENS, D), 0.03, 0.19921875, ((0, 32),))
    log_temp = jnp.clip(jax.random.uniform(key_list[2], (), jnp.float32, 1.0, 2.0), 1.0, 2.0)
    bias = jnp.clip(jax.random.uniform(key_list[3], (), jnp.float32, -2.0, 0.0), -2.0, 0.0)
    return dict(image_emb=image_emb, text_emb=text_emb, log_temp=log_temp, bias=bias)


EPSILON = 1e-06

def unit_rows(embedding):
    values = embedding.astype(jnp.float32)
    scale = lax.rsqrt(lax.optimization_barrier(jnp.sum(values * values, axis=-1, keepdims=True)) + EPSILON)
    return (values * scale, scale)

def to_low(values):
    rounded = lax.optimization_barrier(values.astype(jnp.bfloat16))
    return rounded.astype(jnp.float32)

def reference(image_emb, text_emb, log_temp, bias):
    block_count = TOKENS // ROWS
    image_unit, image_scale = unit_rows(image_emb)
    text_unit, text_scale = unit_rows(text_emb)
    image_blocks = to_low(image_unit).reshape(block_count, ROWS, D)
    text_blocks = to_low(text_unit).reshape(block_count, ROWS, D)
    temper = jnp.exp(log_temp)
    signs = 2.0 * jnp.eye(ROWS, dtype=jnp.float32) - 1.0
    losses = jnp.zeros((block_count, ROWS), jnp.float32)
    grad_img = jnp.zeros((block_count, ROWS, D), jnp.float32)
    grad_txt = jnp.zeros((block_count, ROWS, D), jnp.float32)
    for offset in range(STEPS):
        partner = jnp.roll(text_blocks, offset, axis=0)
        logits = temper * jnp.einsum('bid,bjd->bij', image_blocks, partner, precision=lax.Precision.HIGHEST) + bias
        labels = signs if offset == 0 else -jnp.ones_like(signs)
        losses = losses - lax.optimization_barrier(jnp.sum(jax.nn.log_sigmoid(labels * logits), axis=-1))
        weights = to_low(-labels * jax.nn.sigmoid(-labels * logits) * temper)
        grad_img = grad_img + jnp.einsum('bij,bjd->bid', weights, partner, precision=lax.Precision.HIGHEST)
        term = jnp.einsum('bij,bid->bjd', weights, image_blocks, precision=lax.Precision.HIGHEST)
        grad_txt = grad_txt + jnp.roll(term, -offset, axis=0)
    grad_img = grad_img.reshape(TOKENS, D)
    grad_txt = grad_txt.reshape(TOKENS, D)
    grad_image = image_scale * (grad_img - image_unit * lax.optimization_barrier(jnp.sum(image_unit * grad_img, axis=-1, keepdims=True)))
    grad_text = text_scale * (grad_txt - text_unit * lax.optimization_barrier(jnp.sum(text_unit * grad_txt, axis=-1, keepdims=True)))
    return (losses.reshape(TOKENS), grad_image, grad_text)
```

```python
import functools

import jax
import jax.numpy as jnp
from jax import lax
from jax.experimental import pallas as pl
from jax.experimental.pallas import tpu as pltpu
from jax.sharding import PartitionSpec as P

EPSILON = 1e-06
MESH = pl.DeviceIdType.MESH
CHUNKS = 4
HALVES = 2
NT = (((1,), (1,)), ((), ()))


def row_scale(values):
    return lax.rsqrt(jnp.sum(values * values, axis=-1, keepdims=True) + EPSILON)


def kernel(
    count,
    reps,
    log_temp,
    bias,
    image_emb,
    text_emb,
    loss_out,
    grad_image,
    grad_text,
    image_low,
    text_low,
    texts,
    images,
    loss_acc,
    send_sem,
    text_sem,
    image_sem,
):
    rows, width = image_emb.shape
    piece = rows // CHUNKS
    half = rows // HALVES
    me = lax.axis_index("blk") * reps + lax.axis_index("rep")
    place = lax.rem(me, 4)

    def device(by):
        index = lax.rem(me + by + count, count)
        return (index // reps, lax.rem(index, reps))

    barrier = pltpu.get_barrier_semaphore()
    for by in (-2, -1, 1, 2):
        pl.semaphore_signal(barrier, inc=1, device_id=device(by), device_id_type=MESH)

    def normalise(emb, low, c):
        part = pl.ds(c * piece, piece)
        values = emb[part, :].astype(jnp.float32)
        low[part, :] = (values * row_scale(values)).astype(jnp.bfloat16)

    def copy(kind, c, src, dst, sem, by):
        part = pl.ds(c * piece, piece)
        return pltpu.make_async_remote_copy(
            src_ref=src.at[part, :],
            dst_ref=dst.at[part, :],
            send_sem=send_sem.at[kind, c],
            recv_sem=sem,
            device_id=device(by),
            device_id_type=MESH,
        )

    def text_two(c):
        return copy(0, c, text_low, texts.at[1], text_sem.at[1, c], 2)

    def image_two(c):
        return copy(1, c, image_low, images.at[1], image_sem.at[1, c], -2)

    def text_one(c):
        return copy(2, c, text_low, texts.at[0], text_sem.at[0, c], 1)

    def image_one(c):
        return copy(3, c, image_low, images.at[0], image_sem.at[0, c], -1)

    def text_turn(c):
        return copy(4, c, texts.at[1], texts.at[0], text_sem.at[0, c], -1)

    def image_turn(c):
        return copy(5, c, images.at[1], images.at[0], image_sem.at[0, c], 1)

    def text_three(c):
        return copy(6, c, texts.at[0], texts.at[2], text_sem.at[2, c], 2)

    def image_three(c):
        return copy(7, c, images.at[0], images.at[2], image_sem.at[2, c], -2)

    def got_text(j, c):
        copy(0, c, text_low, texts.at[j], text_sem.at[j, c], 2).wait_recv()

    def got_image(j, c):
        copy(1, c, image_low, images.at[j], image_sem.at[j, c], -2).wait_recv()

    normalise(text_emb, text_low, 0)
    normalise(image_emb, image_low, 0)
    pl.semaphore_wait(barrier, 4)
    for c in range(CHUNKS):
        if c > 0:
            normalise(text_emb, text_low, c)
            normalise(image_emb, image_low, c)

        @pl.when(place != 3)
        def _():
            text_one(c).start()

        @pl.when(place != 0)
        def _():
            image_one(c).start()

        text_two(c).start()
        image_two(c).start()

    temper = jnp.exp(jnp.full((1, half), log_temp[0], jnp.float32))
    slope = 0.5 * temper
    shift = jnp.full((1, half), 0.5 * bias[0], jnp.float32)
    grad_image[...] = jnp.zeros_like(grad_image)
    grad_text[...] = jnp.zeros_like(grad_text)
    loss_acc[...] = jnp.zeros_like(loss_acc)

    def step(own, other, acc, h, diagonal, with_loss):
        block = other[pl.ds(h * half, half), :]

        @pl.loop(0, HALVES)
        def _(m):
            part = pl.ds(pl.multiple_of(m * half, half), half)
            dots = lax.dot_general(own[part, :], block, NT, preferred_element_type=jnp.float32)
            turn = jnp.tanh(dots * slope + shift)
            weights = slope + slope * turn
            other_side = 0.5 - 0.5 * turn
            if diagonal:
                row = lax.broadcasted_iota(jnp.int32, (half, half), 0)
                column = lax.broadcasted_iota(jnp.int32, (half, half), 1)
                positive = row + m * half == column + h * half
                weights = jnp.where(positive, slope * turn - slope, weights)
                other_side = jnp.where(positive, 0.5 + 0.5 * turn, other_side)
            if with_loss:
                product = other_side[:, :128]
                for at in range(128, half, 128):
                    product = product * other_side[:, at : at + 128]
                loss_acc[part, :] -= jnp.log(product)
            acc[part, :] += jnp.dot(
                weights.astype(jnp.bfloat16), block, preferred_element_type=jnp.float32
            )

    def image_step(other, h, diagonal=False):
        step(image_low, other, grad_image, h, diagonal, True)

    def text_step(other, h, diagonal=False):
        step(text_low, other, grad_text, h, diagonal, False)

    def pass_text(c):
        got_text(0, c)
        text_three(c).start()

    def pass_image(c):
        got_image(0, c)
        image_three(c).start()

    def arrivals(c):
        got_text(1, c)

        @pl.when(place == 1)
        def _():
            text_turn(c).start()

        got_image(1, c)

        @pl.when(place == 2)
        def _():
            image_turn(c).start()

        @pl.when(place == 0)
        def _():
            pass_image(c)
            if c > 0:
                pass_text(c - 1)

        @pl.when(place == 3)
        def _():
            pass_text(c)
            if c > 0:
                pass_image(c - 1)

        @pl.when(jnp.logical_and(place != 0, place != 3))
        def _():
            pass_text(c)
            pass_image(c)

    for h in range(HALVES):
        image_step(text_low, h, True)
        text_step(image_low, h, True)
    per = CHUNKS // HALVES
    for h in range(HALVES):
        for c in range(h * per, (h + 1) * per):
            arrivals(c)
        if h == HALVES - 1:

            @pl.when(place == 0)
            def _():
                pass_text(CHUNKS - 1)

            @pl.when(place == 3)
            def _():
                pass_image(CHUNKS - 1)

        image_step(texts.at[1], h)
        text_step(images.at[1], h)
        if h > 0:
            image_step(texts.at[0], h - 1)
            text_step(images.at[0], h - 1)
    image_step(texts.at[0], HALVES - 1)
    text_step(images.at[0], HALVES - 1)
    for h in range(HALVES):
        for c in range(h * per, (h + 1) * per):
            got_text(2, c)
            got_image(2, c)
        image_step(texts.at[2], h)
        text_step(images.at[2], h)

    def finish(emb, acc):
        @pl.loop(0, CHUNKS)
        def _(c):
            part = pl.ds(pl.multiple_of(c * piece, piece), piece)
            values = emb[part, :].astype(jnp.float32)
            scale = row_scale(values)
            unit = values * scale
            grad = acc[part, :]
            acc[part, :] = scale * (grad - unit * jnp.sum(unit * grad, axis=-1, keepdims=True))

    finish(image_emb, grad_image)
    finish(text_emb, grad_text)
    for at in range(rows // 128):
        part = loss_acc[at * 128 : (at + 1) * 128, :]
        loss_out[at : at + 1, :] = jnp.sum(part.T, axis=0, keepdims=True)

    for c in range(CHUNKS):
        text_two(c).wait_send()
        image_two(c).wait_send()
        text_three(c).wait_send()
        image_three(c).wait_send()

        @pl.when(place != 3)
        def _():
            text_one(c).wait_send()

        @pl.when(place != 0)
        def _():
            image_one(c).wait_send()

        @pl.when(place == 1)
        def _():
            text_turn(c).wait_send()

        @pl.when(place == 2)
        def _():
            image_turn(c).wait_send()


def body(count, reps, image_emb, text_emb, log_temp, bias):
    rows, width = image_emb.shape
    vmem = pl.BlockSpec(memory_space=pltpu.VMEM)
    smem = pl.BlockSpec(memory_space=pltpu.SMEM)
    losses, grad_image, grad_text = pl.pallas_call(
        functools.partial(kernel, count, reps),
        out_shape=(
            jax.ShapeDtypeStruct((rows // 128, 128), jnp.float32),
            jax.ShapeDtypeStruct((rows, width), jnp.float32),
            jax.ShapeDtypeStruct((rows, width), jnp.float32),
        ),
        in_specs=[smem, smem, vmem, vmem],
        out_specs=(vmem, vmem, vmem),
        scratch_shapes=[
            pltpu.VMEM((rows, width), jnp.bfloat16),
            pltpu.VMEM((rows, width), jnp.bfloat16),
            pltpu.VMEM((3, rows, width), jnp.bfloat16),
            pltpu.VMEM((3, rows, width), jnp.bfloat16),
            pltpu.VMEM((rows, 128), jnp.float32),
            pltpu.SemaphoreType.DMA((8, CHUNKS)),
            pltpu.SemaphoreType.DMA((3, CHUNKS)),
            pltpu.SemaphoreType.DMA((3, CHUNKS)),
        ],
        compiler_params=pltpu.CompilerParams(
            collective_id=0, has_side_effects=True, vmem_limit_bytes=44 * 1024 * 1024
        ),
        cost_estimate=pl.CostEstimate(
            flops=32 * rows * rows * width,
            bytes_accessed=12 * rows * width,
            transcendentals=14 * rows * rows,
        ),
    )(log_temp.reshape(1), bias.reshape(1), image_emb, text_emb)
    return losses.reshape(rows), grad_image, grad_text


def solution(mesh):
    reps = mesh.shape["rep"]
    count = mesh.shape["blk"] * reps
    return jax.shard_map(
        functools.partial(body, count, reps),
        mesh=mesh,
        in_specs=(P(("blk", "rep"), None), P(("blk", "rep"), None), P(), P()),
        out_specs=(P(("blk", "rep")), P(("blk", "rep"), None), P(("blk", "rep"), None)),
        check_vma=False,
    )
```

```python
import functools

import jax
import jax.numpy as jnp
from jax import lax
from jax.experimental import pallas as pl
from jax.experimental.pallas import tpu as pltpu
from jax.sharding import PartitionSpec as P

EPSILON = 1e-06
MESH = pl.DeviceIdType.MESH
CHUNKS = 4
HALVES = 2
NT = (((1,), (1,)), ((), ()))


def row_scale(values):
    return lax.rsqrt(jnp.sum(values * values, axis=-1, keepdims=True) + EPSILON)


def kernel(
    blocks,
    log_temp,
    bias,
    image_emb,
    text_emb,
    loss_out,
    grad_image,
    grad_text,
    image_held,
    text_held,
    image_low,
    text_low,
    texts,
    images,
    loss_acc,
    fetch_sem,
    send_sem,
    text_sem,
    image_sem,
):
    rows, width = image_emb.shape
    piece = rows // CHUNKS
    half = rows // HALVES
    blk, rep = lax.axis_index("blk"), lax.axis_index("rep")
    ahead = (lax.rem(blk + 1, blocks), rep)
    behind = (lax.rem(blk + blocks - 1, blocks), rep)
    across = (blk, 1 - rep)
    core = lax.rem(blk, 2)

    def chunk(c):
        return pl.ds(c * piece, piece)

    def fetch(kind, emb, held, c):
        return pltpu.make_async_copy(
            emb.at[chunk(c), :], held.at[chunk(c), :], fetch_sem.at[kind, c]
        )

    for c in range(CHUNKS):
        fetch(0, text_emb, text_held, c).start()
        fetch(1, image_emb, image_held, c).start()
    barrier = pltpu.get_barrier_semaphore()
    for other in (ahead, behind, across):
        pl.semaphore_signal(barrier, inc=1, device_id=other, device_id_type=MESH)

    def normalise(held, low, c):
        values = held[chunk(c), :].astype(jnp.float32)
        low[chunk(c), :] = (values * row_scale(values)).astype(jnp.bfloat16)

    def prepare(c):
        fetch(0, text_emb, text_held, c).wait()
        normalise(text_held, text_low, c)
        fetch(1, image_emb, image_held, c).wait()
        normalise(image_held, image_low, c)

    def copy(kind, c, src, dst, sem, to):
        return pltpu.make_async_remote_copy(
            src_ref=src.at[chunk(c), :],
            dst_ref=dst.at[chunk(c), :],
            send_sem=send_sem.at[kind, c],
            recv_sem=sem,
            device_id=to,
            device_id_type=MESH,
        )

    def text_two(c):
        return copy(0, c, text_low, texts.at[1], text_sem.at[1, c], ahead)

    def image_two(c):
        return copy(1, c, image_low, images.at[1], image_sem.at[1, c], behind)

    def text_three(c):
        return copy(2, c, texts.at[0], texts.at[2], text_sem.at[2, c], ahead)

    def image_three(c):
        return copy(3, c, images.at[0], images.at[2], image_sem.at[2, c], behind)

    def text_one(c):
        return copy(4, c, text_low, texts.at[0], text_sem.at[0, c], across)

    def image_turn(c):
        return copy(5, c, images.at[1], images.at[0], image_sem.at[0, c], across)

    def image_one(c):
        return copy(4, c, image_low, images.at[0], image_sem.at[0, c], across)

    def text_turn(c):
        return copy(5, c, texts.at[1], texts.at[0], text_sem.at[0, c], across)

    def got_text(j, c):
        copy(0, c, text_low, texts.at[j], text_sem.at[j, c], ahead).wait_recv()

    def got_image(j, c):
        copy(1, c, image_low, images.at[j], image_sem.at[j, c], behind).wait_recv()

    def pass_text(c):
        got_text(0, c)
        text_three(c).start()

    def pass_image(c):
        got_image(0, c)
        image_three(c).start()

    first, second = core == 0, core == 1
    even, odd = rep == 0, rep == 1

    def on(*conditions):
        return pl.when(functools.reduce(jnp.logical_and, conditions))

    prepare(0)
    pl.semaphore_wait(barrier, 3)
    for c in range(CHUNKS):
        if c > 0:
            prepare(c)
        text_two(c).start()
        image_two(c).start()

        @on(even, second)
        def _():
            text_one(c).start()

        @on(odd, first)
        def _():
            image_one(c).start()

    @on(even, first)
    def _():
        for c in range(CHUNKS):
            got_image(1, c)
            image_turn(c).start()
        for c in range(CHUNKS):
            text_one(c).start()

    @on(odd, second)
    def _():
        for c in range(CHUNKS):
            got_text(1, c)
            text_turn(c).start()
        for c in range(CHUNKS):
            image_one(c).start()

    temper = jnp.exp(jnp.full((1, half), log_temp[0], jnp.float32))
    slope = 0.5 * temper
    shift = jnp.full((1, half), 0.5 * bias[0], jnp.float32)
    grad_image[...] = jnp.zeros_like(grad_image)
    grad_text[...] = jnp.zeros_like(grad_text)
    loss_acc[...] = jnp.zeros_like(loss_acc)

    def step(own, other, acc, h, diagonal, with_loss):
        block = other[pl.ds(h * half, half), :]

        @pl.loop(0, HALVES)
        def _(m):
            part = pl.ds(pl.multiple_of(m * half, half), half)
            dots = lax.dot_general(own[part, :], block, NT, preferred_element_type=jnp.float32)
            turn = jnp.tanh(dots * slope + shift)
            weights = slope + slope * turn
            other_side = 0.5 - 0.5 * turn
            if diagonal:
                row = lax.broadcasted_iota(jnp.int32, (half, half), 0)
                column = lax.broadcasted_iota(jnp.int32, (half, half), 1)
                positive = row + m * half == column + h * half
                weights = jnp.where(positive, slope * turn - slope, weights)
                other_side = jnp.where(positive, 0.5 + 0.5 * turn, other_side)
            if with_loss:
                product = other_side[:, :128]
                for at in range(128, half, 128):
                    product = product * other_side[:, at : at + 128]
                loss_acc[part, :] -= jnp.log(product)
            acc[part, :] += jnp.dot(
                weights.astype(jnp.bfloat16), block, preferred_element_type=jnp.float32
            )

    def image_step(other, h, diagonal=False):
        step(image_low, other, grad_image, h, diagonal, True)

    def text_step(other, h, diagonal=False):
        step(text_low, other, grad_text, h, diagonal, False)

    def early(c):
        @on(first)
        def _():
            pass_image(c)
            got_text(1, c)

        @on(first, odd)
        def _():
            text_turn(c).start()
            got_image(1, c)

        @on(second)
        def _():
            pass_text(c)
            got_image(1, c)

        @on(second, even)
        def _():
            image_turn(c).start()
            got_text(1, c)

    def late(c):
        @on(first)
        def _():
            pass_text(c)

        @on(second)
        def _():
            pass_image(c)

    for h in range(HALVES):
        image_step(text_low, h, True)
        text_step(image_low, h, True)
    per = CHUNKS // HALVES
    for h in range(HALVES):
        for c in range(h * per, (h + 1) * per):
            early(c)
            if c > 0:
                late(c - 1)
            if h > 0 and c == h * per:
                image_step(texts.at[0], h - 1)
                text_step(images.at[0], h - 1)
        image_step(texts.at[1], h)
        text_step(images.at[1], h)
    late(CHUNKS - 1)
    image_step(texts.at[0], HALVES - 1)
    text_step(images.at[0], HALVES - 1)
    for h in range(HALVES):
        for c in range(h * per, (h + 1) * per):
            got_text(2, c)
            got_image(2, c)
        image_step(texts.at[2], h)
        text_step(images.at[2], h)

    def finish(held, acc):
        @pl.loop(0, CHUNKS)
        def _(c):
            part = pl.ds(pl.multiple_of(c * piece, piece), piece)
            values = held[part, :].astype(jnp.float32)
            scale = row_scale(values)
            unit = values * scale
            grad = acc[part, :]
            acc[part, :] = scale * (grad - unit * jnp.sum(unit * grad, axis=-1, keepdims=True))

    finish(image_held, grad_image)
    finish(text_held, grad_text)
    for at in range(rows // 128):
        part = loss_acc[at * 128 : (at + 1) * 128, :]
        loss_out[at : at + 1, :] = jnp.sum(part.T, axis=0, keepdims=True)

    for c in range(CHUNKS):
        text_two(c).wait_send()
        image_two(c).wait_send()
        text_three(c).wait_send()
        image_three(c).wait_send()

        @on(even)
        def _():
            text_one(c).wait_send()
            image_turn(c).wait_send()

        @on(odd)
        def _():
            image_one(c).wait_send()
            text_turn(c).wait_send()


def body(blocks, image_emb, text_emb, log_temp, bias):
    rows, width = image_emb.shape
    vmem = pl.BlockSpec(memory_space=pltpu.VMEM)
    hbm = pl.BlockSpec(memory_space=pltpu.HBM)
    smem = pl.BlockSpec(memory_space=pltpu.SMEM)
    losses, grad_image, grad_text = pl.pallas_call(
        functools.partial(kernel, blocks),
        out_shape=(
            jax.ShapeDtypeStruct((rows // 128, 128), jnp.float32),
            jax.ShapeDtypeStruct((rows, width), jnp.float32),
            jax.ShapeDtypeStruct((rows, width), jnp.float32),
        ),
        in_specs=[smem, smem, hbm, hbm],
        out_specs=(vmem, vmem, vmem),
        scratch_shapes=[
            pltpu.VMEM((rows, width), jnp.bfloat16),
            pltpu.VMEM((rows, width), jnp.bfloat16),
            pltpu.VMEM((rows, width), jnp.bfloat16),
            pltpu.VMEM((rows, width), jnp.bfloat16),
            pltpu.VMEM((3, rows, width), jnp.bfloat16),
            pltpu.VMEM((3, rows, width), jnp.bfloat16),
            pltpu.VMEM((rows, 128), jnp.float32),
            pltpu.SemaphoreType.DMA((2, CHUNKS)),
            pltpu.SemaphoreType.DMA((6, CHUNKS)),
            pltpu.SemaphoreType.DMA((3, CHUNKS)),
            pltpu.SemaphoreType.DMA((3, CHUNKS)),
        ],
        compiler_params=pltpu.CompilerParams(
            collective_id=0, has_side_effects=True, vmem_limit_bytes=44 * 1024 * 1024
        ),
        cost_estimate=pl.CostEstimate(
            flops=32 * rows * rows * width,
            bytes_accessed=12 * rows * width,
            transcendentals=14 * rows * rows,
        ),
    )(log_temp.reshape(1), bias.reshape(1), image_emb, text_emb)
    return losses.reshape(rows), grad_image, grad_text


def solution(mesh):
    if mesh.shape["rep"] != 2 or mesh.shape["blk"] % 2:
        raise ValueError("mesh")
    return jax.shard_map(
        functools.partial(body, mesh.shape["blk"]),
        mesh=mesh,
        in_specs=(P(("blk", "rep"), None), P(("blk", "rep"), None), P(), P()),
        out_specs=(P(("blk", "rep")), P(("blk", "rep"), None), P(("blk", "rep"), None)),
        check_vma=False,
    )
```

```python
import functools

import jax
import jax.numpy as jnp
from jax import lax
from jax.experimental import pallas as pl
from jax.experimental.pallas import tpu as pltpu
from jax.sharding import PartitionSpec as P

EPSILON = 1e-06
MESH = pl.DeviceIdType.MESH
CHUNKS = 4
HALVES = 2
NT = (((1,), (1,)), ((), ()))


def row_scale(values):
    return lax.rsqrt(jnp.sum(values * values, axis=-1, keepdims=True) + EPSILON)


def kernel(
    blocks,
    log_temp,
    bias,
    image_emb,
    text_emb,
    loss_out,
    grads,
    held,
    low,
    came,
    loss_acc,
    fetch_sem,
    send_sem,
    came_sem,
):
    rows, width = image_emb.shape
    piece = rows // CHUNKS
    half = rows // HALVES
    blk, rep = lax.axis_index("blk"), lax.axis_index("rep")
    core = lax.rem(blk, 2)
    mate = (blk + 1 - 2 * core, rep)
    far = (lax.rem(blk + blocks - 1 + 2 * core, blocks), rep)
    across = (blk, 1 - rep)
    outer, inner = 1 - core, core
    straight, turned = rep == outer, rep != outer

    def chunk(c):
        return pl.ds(c * piece, piece)

    def fetch(side, c):
        emb = text_emb if side else image_emb
        return pltpu.make_async_copy(
            emb.at[chunk(c), :], held.at[side, chunk(c), :], fetch_sem.at[side, c]
        )

    for c in range(CHUNKS):
        fetch(0, c).start()
        fetch(1, c).start()
    barrier = pltpu.get_barrier_semaphore()
    for other in (mate, far, across):
        pl.semaphore_signal(barrier, inc=1, device_id=other, device_id_type=MESH)

    def prepare(c):
        for side in range(2):
            fetch(side, c).wait()
            values = held[side, chunk(c), :].astype(jnp.float32)
            low[side, chunk(c), :] = (values * row_scale(values)).astype(jnp.bfloat16)

    def copy(kind, c, src, side, j, to):
        return pltpu.make_async_remote_copy(
            src_ref=src.at[chunk(c), :],
            dst_ref=came.at[side, j, chunk(c), :],
            send_sem=send_sem.at[kind, c],
            recv_sem=came_sem.at[side, j, c],
            device_id=to,
            device_id_type=MESH,
        )

    def far_own(c):
        return copy(0, c, low.at[1 - outer], outer, 1, far)

    def mate_own(c):
        return copy(1, c, low.at[1 - inner], inner, 1, mate)

    def far_pass(c):
        return copy(2, c, came.at[outer, 0], outer, 2, far)

    def mate_pass(c):
        return copy(3, c, came.at[inner, 0], inner, 2, mate)

    def across_own(c):
        return copy(4, c, low.at[1 - rep], rep, 0, across)

    def across_turn(c):
        return copy(5, c, came.at[1 - rep, 1], 1 - rep, 0, across)

    def got(side, j, c):
        copy(0, c, low.at[0], side, j, far).wait_recv()

    prepare(0)
    pl.semaphore_wait(barrier, 3)
    for c in range(CHUNKS):
        if c > 0:
            prepare(c)
        far_own(c).start()
        mate_own(c).start()

        @pl.when(straight)
        def _():
            across_own(c).start()

    @pl.when(turned)
    def _():
        for c in range(CHUNKS):
            got(outer, 1, c)
            across_turn(c).start()

    temper = jnp.exp(jnp.full((1, half), log_temp[0], jnp.float32))
    slope = 0.5 * temper
    shift = jnp.full((1, half), 0.5 * bias[0], jnp.float32)
    grads[...] = jnp.zeros_like(grads)
    loss_acc[...] = jnp.zeros_like(loss_acc)

    def step(side, block, h, diagonal=False):
        @pl.loop(0, HALVES)
        def _(m):
            part = pl.ds(pl.multiple_of(m * half, half), half)
            own = low[side, part, :]
            dots = lax.dot_general(own, block, NT, preferred_element_type=jnp.float32)
            turn = jnp.tanh(dots * slope + shift)
            weights = slope + slope * turn
            other_side = 0.5 - 0.5 * turn
            if diagonal:
                row = lax.broadcasted_iota(jnp.int32, (half, half), 0)
                column = lax.broadcasted_iota(jnp.int32, (half, half), 1)
                positive = row + m * half == column + h * half
                weights = jnp.where(positive, slope * turn - slope, weights)
                other_side = jnp.where(positive, 0.5 + 0.5 * turn, other_side)
            product = other_side[:, :128]
            for at in range(128, half, 128):
                product = product * other_side[:, at : at + 128]
            loss_acc[side, part, :] -= jnp.log(product)
            grads[side, part, :] += jnp.dot(
                weights.astype(jnp.bfloat16), block, preferred_element_type=jnp.float32
            )

    def own_step(side):
        for h in range(HALVES):
            step(side, low[1 - side, pl.ds(h * half, half), :], h, True)

    def came_step(side, j, h):
        step(side, came[side, j, pl.ds(h * half, half), :], h)

    per = CHUNKS // HALVES

    def early(c):
        got(outer, 0, c)
        far_pass(c).start()
        got(inner, 1, c)

        @pl.when(straight)
        def _():
            across_turn(c).start()
            got(outer, 1, c)

        @pl.when(turned)
        def _():
            across_own(c).start()

    def late(c):
        got(inner, 0, c)
        mate_pass(c).start()

    own_step(0)
    early(0)
    own_step(1)
    early(1)
    came_step(outer, 1, 0)
    came_step(inner, 1, 0)
    early(2)
    came_step(outer, 0, 0)
    early(3)
    came_step(outer, 1, 1)
    came_step(inner, 1, 1)
    came_step(outer, 0, 1)
    for h in range(HALVES):
        pieces = range(h * per, (h + 1) * per)
        for c in pieces:
            late(c)
        came_step(inner, 0, h)
        for c in pieces:
            got(inner, 2, c)
        came_step(inner, 2, h)
        for c in pieces:
            got(outer, 2, c)
        came_step(outer, 2, h)

    for side in range(2):

        @pl.loop(0, CHUNKS)
        def _(c):
            part = pl.ds(pl.multiple_of(c * piece, piece), piece)
            values = held[side, part, :].astype(jnp.float32)
            scale = row_scale(values)
            unit = values * scale
            grad = grads[side, part, :]
            grads[side, part, :] = scale * (
                grad - unit * jnp.sum(unit * grad, axis=-1, keepdims=True)
            )

    for at in range(rows // 128):
        part = loss_acc[0, at * 128 : (at + 1) * 128, :]
        loss_out[at : at + 1, :] = jnp.sum(part.T, axis=0, keepdims=True)

    for c in range(CHUNKS):
        for sent in (far_own, mate_own, far_pass, mate_pass, across_own, across_turn):
            sent(c).wait_send()


def body(blocks, image_emb, text_emb, log_temp, bias):
    rows, width = image_emb.shape
    vmem = pl.BlockSpec(memory_space=pltpu.VMEM)
    hbm = pl.BlockSpec(memory_space=pltpu.HBM)
    smem = pl.BlockSpec(memory_space=pltpu.SMEM)
    losses, grads = pl.pallas_call(
        functools.partial(kernel, blocks),
        out_shape=(
            jax.ShapeDtypeStruct((rows // 128, 128), jnp.float32),
            jax.ShapeDtypeStruct((2, rows, width), jnp.float32),
        ),
        in_specs=[smem, smem, hbm, hbm],
        out_specs=(vmem, vmem),
        scratch_shapes=[
            pltpu.VMEM((2, rows, width), jnp.bfloat16),
            pltpu.VMEM((2, rows, width), jnp.bfloat16),
            pltpu.VMEM((2, 3, rows, width), jnp.bfloat16),
            pltpu.VMEM((2, rows, 128), jnp.float32),
            pltpu.SemaphoreType.DMA((2, CHUNKS)),
            pltpu.SemaphoreType.DMA((6, CHUNKS)),
            pltpu.SemaphoreType.DMA((2, 3, CHUNKS)),
        ],
        compiler_params=pltpu.CompilerParams(
            collective_id=0, has_side_effects=True, vmem_limit_bytes=44 * 1024 * 1024
        ),
        cost_estimate=pl.CostEstimate(
            flops=32 * rows * rows * width,
            bytes_accessed=12 * rows * width,
            transcendentals=14 * rows * rows,
        ),
    )(log_temp.reshape(1), bias.reshape(1), image_emb, text_emb)
    return losses.reshape(rows), grads[0], grads[1]


def solution(mesh):
    if mesh.shape["rep"] != 2 or mesh.shape["blk"] % 2:
        raise ValueError("mesh")
    return jax.shard_map(
        functools.partial(body, mesh.shape["blk"]),
        mesh=mesh,
        in_specs=(P(("blk", "rep"), None), P(("blk", "rep"), None), P(), P()),
        out_specs=(P(("blk", "rep")), P(("blk", "rep"), None), P(("blk", "rep"), None)),
        check_vma=False,
    )
```

```python
import functools

import jax
import jax.numpy as jnp
from jax import lax
from jax.experimental import pallas as pl
from jax.experimental.pallas import tpu as pltpu
from jax.sharding import PartitionSpec as P

EPSILON = 1e-06
MESH = pl.DeviceIdType.MESH
CHUNKS = 8
PIECES = 8
HALVES = 2
NT = (((1,), (1,)), ((), ()))


def row_scale(values):
    return lax.rsqrt(jnp.sum(values * values, axis=-1, keepdims=True) + EPSILON)


def kernel(
    blocks,
    log_temp,
    bias,
    image_emb,
    text_emb,
    loss_acc,
    grads,
    held,
    low,
    came,
    fetch_sem,
    send_sem,
    came_sem,
):
    rows, width = image_emb.shape
    piece = rows // CHUNKS
    half = rows // HALVES
    blk, rep = lax.axis_index("blk"), lax.axis_index("rep")
    core = lax.rem(blk, 2)
    mate = (blk + 1 - 2 * core, rep)
    far = (lax.rem(blk + blocks - 1 + 2 * core, blocks), rep)
    across = (blk, 1 - rep)
    outer, inner = 1 - core, core
    straight, turned = rep == outer, rep != outer

    def chunk(c):
        return pl.ds(c * piece, piece)

    def fetch(side, c):
        emb = text_emb if side else image_emb
        return pltpu.make_async_copy(
            emb.at[chunk(c), :], held.at[side, chunk(c), :], fetch_sem.at[side, c]
        )

    for c in range(CHUNKS):
        fetch(0, c).start()
        fetch(1, c).start()
    barrier = pltpu.get_barrier_semaphore()
    for other in (mate, far, across):
        pl.semaphore_signal(barrier, inc=1, device_id=other, device_id_type=MESH)

    def prepare(c):
        for side in range(2):
            fetch(side, c).wait()
            values = held[side, chunk(c), :].astype(jnp.float32)
            low[side, chunk(c), :] = (values * row_scale(values)).astype(jnp.bfloat16)

    def copy(kind, c, src, side, j, to):
        return pltpu.make_async_remote_copy(
            src_ref=src.at[chunk(c), :],
            dst_ref=came.at[side, j, chunk(c), :],
            send_sem=send_sem.at[kind, c],
            recv_sem=came_sem.at[side, j, c],
            device_id=to,
            device_id_type=MESH,
        )

    def far_own(c):
        return copy(0, c, low.at[1 - outer], outer, 1, far)

    def mate_own(c):
        return copy(1, c, low.at[1 - inner], inner, 1, mate)

    def far_pass(c):
        return copy(2, c, came.at[outer, 0], outer, 2, far)

    def mate_pass(c):
        return copy(3, c, came.at[inner, 0], inner, 2, mate)

    def across_own(c):
        return copy(4, c, low.at[1 - rep], rep, 0, across)

    def across_turn(c):
        return copy(5, c, came.at[1 - rep, 1], 1 - rep, 0, across)

    def got(side, j, c):
        copy(0, c, low.at[0], side, j, far).wait_recv()

    prepare(0)
    pl.semaphore_wait(barrier, 3)
    for c in range(CHUNKS):
        if c > 0:
            prepare(c)
        far_own(c).start()
        mate_own(c).start()

        @pl.when(straight)
        def _():
            across_own(c).start()

    @pl.when(turned)
    def _():
        for c in range(CHUNKS):
            got(outer, 1, c)
            across_turn(c).start()

    temper = jnp.exp(jnp.full((1, half), log_temp[0], jnp.float32))
    slope = 0.5 * temper
    shift = jnp.full((1, half), 0.5 * bias[0], jnp.float32)
    grads[...] = jnp.zeros_like(grads)
    loss_acc[...] = jnp.zeros_like(loss_acc)

    def step(side, block, h, diagonal=False):
        @pl.loop(0, HALVES)
        def _(m):
            part = pl.ds(pl.multiple_of(m * half, half), half)
            own = low[side, part, :]
            dots = lax.dot_general(own, block, NT, preferred_element_type=jnp.float32)
            turn = jnp.tanh(dots * slope + shift)
            weights = slope + slope * turn
            other_side = 0.5 - 0.5 * turn
            if diagonal:
                row = lax.broadcasted_iota(jnp.int32, (half, half), 0)
                column = lax.broadcasted_iota(jnp.int32, (half, half), 1)
                positive = row + m * half == column + h * half
                weights = jnp.where(positive, slope * turn - slope, weights)
                other_side = jnp.where(positive, 0.5 + 0.5 * turn, other_side)
            product = other_side[:, :128]
            for at in range(128, half, 128):
                product = product * other_side[:, at : at + 128]
            loss_acc[side, part, :] -= jnp.log(product)
            grads[side, part, :] += jnp.dot(
                weights.astype(jnp.bfloat16), block, preferred_element_type=jnp.float32
            )

    def own_step(side):
        for h in range(HALVES):
            step(side, low[1 - side, pl.ds(h * half, half), :], h, True)

    def came_step(side, j, h):
        step(side, came[side, j, pl.ds(h * half, half), :], h)

    per = CHUNKS // HALVES

    def early(quarter):
        for c in range(quarter * CHUNKS // 4, (quarter + 1) * CHUNKS // 4):
            early_chunk(c)

    def early_chunk(c):
        got(outer, 0, c)
        far_pass(c).start()
        got(inner, 1, c)

        @pl.when(straight)
        def _():
            across_turn(c).start()
            got(outer, 1, c)

        @pl.when(turned)
        def _():
            across_own(c).start()

    def late(c):
        got(inner, 0, c)
        mate_pass(c).start()

    own_step(0)
    early(0)
    own_step(1)
    early(1)
    came_step(outer, 1, 0)
    came_step(inner, 1, 0)
    early(2)
    came_step(outer, 0, 0)
    early(3)
    came_step(outer, 1, 1)
    came_step(inner, 1, 1)
    came_step(outer, 0, 1)
    for h in range(HALVES):
        pieces = range(h * per, (h + 1) * per)
        for c in pieces:
            late(c)
        came_step(inner, 0, h)
        for c in pieces:
            got(inner, 2, c)
        came_step(inner, 2, h)
        for c in pieces:
            got(outer, 2, c)
        came_step(outer, 2, h)

    for c in range(CHUNKS):
        for sent in (far_own, mate_own, far_pass, mate_pass, across_own, across_turn):
            sent(c).wait_send()


def finish(loss_acc, grads, image_emb, text_emb, loss_out, image_out, text_out, loss, done, sem, loss_sem):
    rows = grads.shape[1]
    piece = rows // PIECES

    def store(side, c):
        part = pl.ds(c * piece, piece)
        out = text_out if side else image_out
        return pltpu.make_async_copy(done.at[side, part, :], out.at[part, :], sem.at[side, c])

    def store_loss():
        return pltpu.make_async_copy(loss, loss_out, loss_sem)

    for c in range(PIECES):
        part = pl.ds(c * piece, piece)
        for side in range(2):
            emb = text_emb if side else image_emb
            values = emb[part, :].astype(jnp.float32)
            scale = row_scale(values)
            unit = values * scale
            grad = grads[side, part, :]
            along = jnp.sum(unit * grad, axis=-1, keepdims=True)
            done[side, part, :] = scale * (grad - unit * along)
            store(side, c).start()
    for at in range(rows // 128):
        part = loss_acc[0, at * 128 : (at + 1) * 128, :]
        loss[at : at + 1, :] = jnp.sum(part.T, axis=0, keepdims=True)
    store_loss().start()
    for c in range(PIECES):
        for side in range(2):
            store(side, c).wait()
    store_loss().wait()


def body(blocks, image_emb, text_emb, log_temp, bias):
    rows, width = image_emb.shape
    vmem = pl.BlockSpec(memory_space=pltpu.VMEM)
    hbm = pl.BlockSpec(memory_space=pltpu.HBM)
    smem = pl.BlockSpec(memory_space=pltpu.SMEM)
    loss_acc, grads = pl.pallas_call(
        functools.partial(kernel, blocks),
        out_shape=(
            jax.ShapeDtypeStruct((2, rows, 128), jnp.float32),
            jax.ShapeDtypeStruct((2, rows, width), jnp.float32),
        ),
        in_specs=[smem, smem, hbm, hbm],
        out_specs=(vmem, vmem),
        scratch_shapes=[
            pltpu.VMEM((2, rows, width), jnp.bfloat16),
            pltpu.VMEM((2, rows, width), jnp.bfloat16),
            pltpu.VMEM((2, 3, rows, width), jnp.bfloat16),
            pltpu.SemaphoreType.DMA((2, CHUNKS)),
            pltpu.SemaphoreType.DMA((6, CHUNKS)),
            pltpu.SemaphoreType.DMA((2, 3, CHUNKS)),
        ],
        compiler_params=pltpu.CompilerParams(
            collective_id=0, has_side_effects=True, vmem_limit_bytes=44 * 1024 * 1024
        ),
        cost_estimate=pl.CostEstimate(
            flops=32 * rows * rows * width,
            bytes_accessed=12 * rows * width,
            transcendentals=14 * rows * rows,
        ),
    )(log_temp.reshape(1), bias.reshape(1), image_emb, text_emb)
    losses, grad_image, grad_text = pl.pallas_call(
        finish,
        out_shape=(
            jax.ShapeDtypeStruct((rows // 128, 128), jnp.float32),
            jax.ShapeDtypeStruct((rows, width), jnp.float32),
            jax.ShapeDtypeStruct((rows, width), jnp.float32),
        ),
        in_specs=[vmem] * 4,
        out_specs=(hbm, hbm, hbm),
        scratch_shapes=[
            pltpu.VMEM((rows // 128, 128), jnp.float32),
            pltpu.VMEM((2, rows, width), jnp.float32),
            pltpu.SemaphoreType.DMA((2, PIECES)),
            pltpu.SemaphoreType.DMA,
        ],
        compiler_params=pltpu.CompilerParams(vmem_limit_bytes=20 * 1024 * 1024),
        cost_estimate=pl.CostEstimate(
            flops=16 * rows * width, bytes_accessed=8 * rows * width, transcendentals=2 * rows
        ),
    )(loss_acc, grads, image_emb, text_emb)
    return losses.reshape(rows), grad_image, grad_text


def solution(mesh):
    if mesh.shape["rep"] != 2 or mesh.shape["blk"] % 2:
        raise ValueError("mesh")
    return jax.shard_map(
        functools.partial(body, mesh.shape["blk"]),
        mesh=mesh,
        in_specs=(P(("blk", "rep"), None), P(("blk", "rep"), None), P(), P()),
        out_specs=(P(("blk", "rep")), P(("blk", "rep"), None), P(("blk", "rep"), None)),
        check_vma=False,
    )
```

```python
import functools

import jax
import jax.numpy as jnp
from jax import lax
from jax.experimental import pallas as pl
from jax.experimental.pallas import tpu as pltpu
from jax.sharding import PartitionSpec as P

EPSILON = 1e-06
MESH = pl.DeviceIdType.MESH
CHUNKS = 4
PIECES = 8
HALVES = 2
NT = (((1,), (1,)), ((), ()))


def row_scale(values):
    return lax.rsqrt(jnp.sum(values * values, axis=-1, keepdims=True) + EPSILON)


def kernel(
    blocks,
    log_temp,
    bias,
    image_emb,
    text_emb,
    loss_acc,
    grads,
    held,
    low,
    came,
    fetch_sem,
    send_sem,
    came_sem,
):
    rows, width = image_emb.shape
    piece = rows // CHUNKS
    half = rows // HALVES
    blk, rep = lax.axis_index("blk"), lax.axis_index("rep")
    core = lax.rem(blk, 2)
    mate = (blk + 1 - 2 * core, rep)
    far = (lax.rem(blk + blocks - 1 + 2 * core, blocks), rep)
    across = (blk, 1 - rep)
    outer, inner = 1 - core, core
    straight, turned = rep == outer, rep != outer

    def chunk(c):
        return pl.ds(c * piece, piece)

    def fetch(side, c):
        emb = text_emb if side else image_emb
        return pltpu.make_async_copy(
            emb.at[chunk(c), :], held.at[side, chunk(c), :], fetch_sem.at[side, c]
        )

    for c in range(CHUNKS):
        fetch(0, c).start()
        fetch(1, c).start()
    barrier = pltpu.get_barrier_semaphore()
    for other in (mate, far, across):
        pl.semaphore_signal(barrier, inc=1, device_id=other, device_id_type=MESH)

    def prepare(c):
        for side in range(2):
            fetch(side, c).wait()
            values = held[side, chunk(c), :].astype(jnp.float32)
            low[side, chunk(c), :] = (values * row_scale(values)).astype(jnp.bfloat16)

    def copy(kind, c, src, side, j, to):
        return pltpu.make_async_remote_copy(
            src_ref=src.at[chunk(c), :],
            dst_ref=came.at[side, j, chunk(c), :],
            send_sem=send_sem.at[kind, c],
            recv_sem=came_sem.at[side, j, c],
            device_id=to,
            device_id_type=MESH,
        )

    def far_own(c):
        return copy(0, c, low.at[1 - outer], outer, 1, far)

    def mate_own(c):
        return copy(1, c, low.at[1 - inner], inner, 1, mate)

    def far_pass(c):
        return copy(2, c, came.at[outer, 0], outer, 2, far)

    def mate_pass(c):
        return copy(3, c, came.at[inner, 0], inner, 2, mate)

    def across_own(c):
        return copy(4, c, low.at[1 - rep], rep, 0, across)

    def across_turn(c):
        return copy(5, c, came.at[1 - rep, 1], 1 - rep, 0, across)

    def got(side, j, c):
        copy(0, c, low.at[0], side, j, far).wait_recv()

    prepare(0)
    pl.semaphore_wait(barrier, 3)
    for c in range(CHUNKS):
        if c > 0:
            prepare(c)
        far_own(c).start()
        mate_own(c).start()

        @pl.when(straight)
        def _():
            across_own(c).start()

    @pl.when(turned)
    def _():
        for c in range(CHUNKS):
            got(outer, 1, c)
            across_turn(c).start()

    temper = jnp.exp(jnp.full((1, half), log_temp[0], jnp.float32))
    slope = 0.5 * temper
    shift = jnp.full((1, half), 0.5 * bias[0], jnp.float32)
    grads[...] = jnp.zeros_like(grads)
    loss_acc[...] = jnp.zeros_like(loss_acc)

    def step(side, block, h, diagonal=False):
        dots = lax.dot_general(low[side], block, NT, preferred_element_type=jnp.float32)
        turn = jnp.tanh(dots * slope + shift)
        weights = slope + slope * turn
        other_side = 1.0 - turn
        if diagonal:
            row = lax.broadcasted_iota(jnp.int32, (rows, half), 0)
            column = lax.broadcasted_iota(jnp.int32, (rows, half), 1)
            positive = row == column + h * half
            weights = jnp.where(positive, slope * turn - slope, weights)
            other_side = jnp.where(positive, 1.0 + turn, other_side)
        product = 1.0
        for at in range(0, half, 128):
            product = product * (0.5 * other_side[:, at : at + 128])
        loss_acc[side] -= jnp.log(product)
        grads[side] += jnp.dot(
            weights.astype(jnp.bfloat16), block, preferred_element_type=jnp.float32
        )

    def own_step(side):
        for h in range(HALVES):
            step(side, low[1 - side, pl.ds(h * half, half), :], h, True)

    def came_step(side, j, h):
        step(side, came[side, j, pl.ds(h * half, half), :], h)

    per = CHUNKS // HALVES

    def early(quarter):
        for c in range(quarter * CHUNKS // 4, (quarter + 1) * CHUNKS // 4):
            early_chunk(c)

    def early_chunk(c):
        got(outer, 0, c)
        far_pass(c).start()
        got(inner, 1, c)

        @pl.when(straight)
        def _():
            across_turn(c).start()
            got(outer, 1, c)

        @pl.when(turned)
        def _():
            across_own(c).start()

    def late(c):
        got(inner, 0, c)
        mate_pass(c).start()

    own_step(0)
    early(0)
    own_step(1)
    early(1)
    came_step(outer, 1, 0)
    came_step(inner, 1, 0)
    early(2)
    came_step(outer, 0, 0)
    early(3)
    for c in range(per):
        late(c)
    came_step(outer, 1, 1)
    came_step(inner, 1, 1)
    came_step(outer, 0, 1)
    came_step(inner, 0, 0)
    for c in range(per, CHUNKS):
        late(c)

    def last_step(side, h):
        for c in range(h * per, (h + 1) * per):
            got(side, 2, c)
        came_step(side, 2, h)

    last_step(inner, 0)
    last_step(outer, 0)
    came_step(inner, 0, 1)
    last_step(inner, 1)
    last_step(outer, 1)

    for c in range(CHUNKS):
        for sent in (far_own, mate_own, far_pass, mate_pass, across_own, across_turn):
            sent(c).wait_send()


def finish(loss_acc, grads, image_emb, text_emb, loss_out, image_out, text_out, loss, done, sem, loss_sem):
    rows = grads.shape[1]
    piece = rows // PIECES

    def store(side, c):
        part = pl.ds(c * piece, piece)
        out = text_out if side else image_out
        return pltpu.make_async_copy(done.at[side, part, :], out.at[part, :], sem.at[side, c])

    def store_loss():
        return pltpu.make_async_copy(loss, loss_out, loss_sem)

    for c in range(PIECES):
        part = pl.ds(c * piece, piece)
        for side in range(2):
            emb = text_emb if side else image_emb
            values = emb[part, :].astype(jnp.float32)
            scale = row_scale(values)
            unit = values * scale
            grad = grads[side, part, :]
            along = jnp.sum(unit * grad, axis=-1, keepdims=True)
            done[side, part, :] = scale * (grad - unit * along)
            store(side, c).start()
    for at in range(rows // 128):
        part = loss_acc[0, at * 128 : (at + 1) * 128, :]
        loss[at : at + 1, :] = jnp.sum(part.T, axis=0, keepdims=True)
    store_loss().start()
    for c in range(PIECES):
        for side in range(2):
            store(side, c).wait()
    store_loss().wait()


def body(blocks, image_emb, text_emb, log_temp, bias):
    rows, width = image_emb.shape
    vmem = pl.BlockSpec(memory_space=pltpu.VMEM)
    hbm = pl.BlockSpec(memory_space=pltpu.HBM)
    smem = pl.BlockSpec(memory_space=pltpu.SMEM)
    loss_acc, grads = pl.pallas_call(
        functools.partial(kernel, blocks),
        out_shape=(
            jax.ShapeDtypeStruct((2, rows, 128), jnp.float32),
            jax.ShapeDtypeStruct((2, rows, width), jnp.float32),
        ),
        in_specs=[smem, smem, hbm, hbm],
        out_specs=(vmem, vmem),
        scratch_shapes=[
            pltpu.VMEM((2, rows, width), jnp.bfloat16),
            pltpu.VMEM((2, rows, width), jnp.bfloat16),
            pltpu.VMEM((2, 3, rows, width), jnp.bfloat16),
            pltpu.SemaphoreType.DMA((2, CHUNKS)),
            pltpu.SemaphoreType.DMA((6, CHUNKS)),
            pltpu.SemaphoreType.DMA((2, 3, CHUNKS)),
        ],
        compiler_params=pltpu.CompilerParams(
            collective_id=0, has_side_effects=True, vmem_limit_bytes=44 * 1024 * 1024
        ),
        cost_estimate=pl.CostEstimate(
            flops=32 * rows * rows * width,
            bytes_accessed=12 * rows * width,
            transcendentals=14 * rows * rows,
        ),
    )(log_temp.reshape(1), bias.reshape(1), image_emb, text_emb)
    losses, grad_image, grad_text = pl.pallas_call(
        finish,
        out_shape=(
            jax.ShapeDtypeStruct((rows // 128, 128), jnp.float32),
            jax.ShapeDtypeStruct((rows, width), jnp.float32),
            jax.ShapeDtypeStruct((rows, width), jnp.float32),
        ),
        in_specs=[vmem] * 4,
        out_specs=(hbm, hbm, hbm),
        scratch_shapes=[
            pltpu.VMEM((rows // 128, 128), jnp.float32),
            pltpu.VMEM((2, rows, width), jnp.float32),
            pltpu.SemaphoreType.DMA((2, PIECES)),
            pltpu.SemaphoreType.DMA,
        ],
        compiler_params=pltpu.CompilerParams(vmem_limit_bytes=20 * 1024 * 1024),
        cost_estimate=pl.CostEstimate(
            flops=16 * rows * width, bytes_accessed=8 * rows * width, transcendentals=2 * rows
        ),
    )(loss_acc, grads, image_emb, text_emb)
    return losses.reshape(rows), grad_image, grad_text


def solution(mesh):
    if mesh.shape["rep"] != 2 or mesh.shape["blk"] % 2:
        raise ValueError("mesh")
    return jax.shard_map(
        functools.partial(body, mesh.shape["blk"]),
        mesh=mesh,
        in_specs=(P(("blk", "rep"), None), P(("blk", "rep"), None), P(), P()),
        out_specs=(P(("blk", "rep")), P(("blk", "rep"), None), P(("blk", "rep"), None)),
        check_vma=False,
    )
```

```python
import functools

import jax
import jax.numpy as jnp
from jax import lax
from jax.experimental import pallas as pl
from jax.experimental.pallas import tpu as pltpu
from jax.sharding import PartitionSpec as P

EPSILON = 1e-06
MESH = pl.DeviceIdType.MESH
CHUNKS = 4
PIECES = 8
HALVES = 2
NT = (((1,), (1,)), ((), ()))


def row_scale(values):
    return lax.rsqrt(jnp.sum(values * values, axis=-1, keepdims=True) + EPSILON)


def kernel(
    blocks,
    log_temp,
    bias,
    image_emb,
    text_emb,
    loss_acc,
    grads,
    held,
    low,
    came,
    fetch_sem,
    send_sem,
    came_sem,
):
    rows, width = image_emb.shape
    piece = rows // CHUNKS
    half = rows // HALVES
    blk, rep = lax.axis_index("blk"), lax.axis_index("rep")
    core = lax.rem(blk, 2)
    mate = (blk + 1 - 2 * core, rep)
    far = (lax.rem(blk + blocks - 1 + 2 * core, blocks), rep)
    across = (blk, 1 - rep)
    outer, inner = 1 - core, core
    straight, turned = rep == outer, rep != outer

    def chunk(c):
        return pl.ds(c * piece, piece)

    def fetch(side, c):
        emb = text_emb if side else image_emb
        return pltpu.make_async_copy(
            emb.at[chunk(c), :], held.at[side, chunk(c), :], fetch_sem.at[side, c]
        )

    for c in range(CHUNKS):
        fetch(0, c).start()
        fetch(1, c).start()
    barrier = pltpu.get_barrier_semaphore()
    for other in (mate, far, across):
        pl.semaphore_signal(barrier, inc=1, device_id=other, device_id_type=MESH)

    def prepare(c):
        for side in range(2):
            fetch(side, c).wait()
            values = held[side, chunk(c), :].astype(jnp.float32)
            low[side, chunk(c), :] = (values * row_scale(values)).astype(jnp.bfloat16)

    def copy(kind, c, src, side, j, to):
        return pltpu.make_async_remote_copy(
            src_ref=src.at[chunk(c), :],
            dst_ref=came.at[side, j, chunk(c), :],
            send_sem=send_sem.at[kind, c],
            recv_sem=came_sem.at[side, j, c],
            device_id=to,
            device_id_type=MESH,
        )

    def far_own(c):
        return copy(0, c, low.at[1 - outer], outer, 1, far)

    def mate_own(c):
        return copy(1, c, low.at[1 - inner], inner, 1, mate)

    def far_pass(c):
        return copy(2, c, came.at[outer, 0], outer, 2, far)

    def mate_pass(c):
        return copy(3, c, came.at[inner, 0], inner, 2, mate)

    def across_own(c):
        return copy(4, c, low.at[1 - rep], rep, 0, across)

    def across_turn(c):
        return copy(5, c, came.at[1 - rep, 1], 1 - rep, 0, across)

    def got(side, j, c):
        copy(0, c, low.at[0], side, j, far).wait_recv()

    prepare(0)
    pl.semaphore_wait(barrier, 3)
    for c in range(CHUNKS):
        if c > 0:
            prepare(c)
        far_own(c).start()
        mate_own(c).start()

        @pl.when(straight)
        def _():
            across_own(c).start()

    @pl.when(turned)
    def _():
        for c in range(CHUNKS):
            got(outer, 1, c)
            across_turn(c).start()

    temper = jnp.exp(jnp.full((1, half), log_temp[0], jnp.float32))
    slope = 0.5 * temper
    shift = jnp.full((1, half), 0.5 * bias[0], jnp.float32)
    grads[...] = jnp.zeros_like(grads)
    loss_acc[...] = jnp.zeros_like(loss_acc)

    def step(side, block, h, diagonal=False):
        dots = lax.dot_general(low[side], block, NT, preferred_element_type=jnp.float32)
        turn = jnp.tanh(dots * slope + shift)
        weights = slope + slope * turn
        other_side = 1.0 - turn
        if diagonal:
            row = lax.broadcasted_iota(jnp.int32, (rows, half), 0)
            column = lax.broadcasted_iota(jnp.int32, (rows, half), 1)
            positive = row == column + h * half
            weights = jnp.where(positive, slope * turn - slope, weights)
            other_side = jnp.where(positive, 1.0 + turn, other_side)
        product = 1.0
        for at in range(0, half, 128):
            product = product * (0.5 * other_side[:, at : at + 128])
        loss_acc[side] -= jnp.log(product)
        grads[side] += jnp.dot(
            weights.astype(jnp.bfloat16), block, preferred_element_type=jnp.float32
        )

    def own_step(side):
        for h in range(HALVES):
            step(side, low[1 - side, pl.ds(h * half, half), :], h, True)

    def came_step(side, j, h):
        step(side, came[side, j, pl.ds(h * half, half), :], h)

    per = CHUNKS // HALVES

    def early(c):
        got(inner, 1, c)

        @pl.when(straight)
        def _():
            across_turn(c).start()
            got(outer, 1, c)

    def forward(c):
        got(outer, 0, c)
        far_pass(c).start()

    def late(c):
        got(inner, 0, c)
        mate_pass(c).start()

    own_step(0)
    early(0)
    own_step(1)
    early(1)
    came_step(outer, 1, 0)
    came_step(inner, 1, 0)
    early(2)
    early(3)

    @pl.when(turned)
    def _():
        for c in range(CHUNKS):
            across_own(c).start()

    forward(0)
    forward(1)
    came_step(outer, 1, 1)
    forward(2)
    came_step(inner, 1, 1)
    forward(3)
    came_step(outer, 0, 0)
    came_step(outer, 0, 1)
    late(0)
    late(1)
    came_step(inner, 0, 0)

    def last_step(side, h):
        for c in range(h * per, (h + 1) * per):
            got(side, 2, c)
        came_step(side, 2, h)

    last_step(outer, 0)
    late(2)
    late(3)
    last_step(inner, 0)
    came_step(inner, 0, 1)
    last_step(inner, 1)
    last_step(outer, 1)

    for c in range(CHUNKS):
        for sent in (far_own, mate_own, far_pass, mate_pass, across_own, across_turn):
            sent(c).wait_send()


def finish(loss_acc, grads, image_emb, text_emb, loss_out, image_out, text_out, loss, done, sem, loss_sem):
    rows = grads.shape[1]
    piece = rows // PIECES

    def store(side, c):
        part = pl.ds(c * piece, piece)
        out = text_out if side else image_out
        return pltpu.make_async_copy(done.at[side, part, :], out.at[part, :], sem.at[side, c])

    def store_loss():
        return pltpu.make_async_copy(loss, loss_out, loss_sem)

    for c in range(PIECES):
        part = pl.ds(c * piece, piece)
        for side in range(2):
            emb = text_emb if side else image_emb
            values = emb[part, :].astype(jnp.float32)
            scale = row_scale(values)
            unit = values * scale
            grad = grads[side, part, :]
            along = jnp.sum(unit * grad, axis=-1, keepdims=True)
            done[side, part, :] = scale * (grad - unit * along)
            store(side, c).start()
    for at in range(rows // 128):
        part = loss_acc[0, at * 128 : (at + 1) * 128, :]
        loss[at : at + 1, :] = jnp.sum(part.T, axis=0, keepdims=True)
    store_loss().start()
    for c in range(PIECES):
        for side in range(2):
            store(side, c).wait()
    store_loss().wait()


def body(blocks, image_emb, text_emb, log_temp, bias):
    rows, width = image_emb.shape
    vmem = pl.BlockSpec(memory_space=pltpu.VMEM)
    hbm = pl.BlockSpec(memory_space=pltpu.HBM)
    smem = pl.BlockSpec(memory_space=pltpu.SMEM)
    loss_acc, grads = pl.pallas_call(
        functools.partial(kernel, blocks),
        out_shape=(
            jax.ShapeDtypeStruct((2, rows, 128), jnp.float32),
            jax.ShapeDtypeStruct((2, rows, width), jnp.float32),
        ),
        in_specs=[smem, smem, hbm, hbm],
        out_specs=(vmem, vmem),
        scratch_shapes=[
            pltpu.VMEM((2, rows, width), jnp.bfloat16),
            pltpu.VMEM((2, rows, width), jnp.bfloat16),
            pltpu.VMEM((2, 3, rows, width), jnp.bfloat16),
            pltpu.SemaphoreType.DMA((2, CHUNKS)),
            pltpu.SemaphoreType.DMA((6, CHUNKS)),
            pltpu.SemaphoreType.DMA((2, 3, CHUNKS)),
        ],
        compiler_params=pltpu.CompilerParams(
            collective_id=0, has_side_effects=True, vmem_limit_bytes=44 * 1024 * 1024
        ),
        cost_estimate=pl.CostEstimate(
            flops=32 * rows * rows * width,
            bytes_accessed=12 * rows * width,
            transcendentals=14 * rows * rows,
        ),
    )(log_temp.reshape(1), bias.reshape(1), image_emb, text_emb)
    losses, grad_image, grad_text = pl.pallas_call(
        finish,
        out_shape=(
            jax.ShapeDtypeStruct((rows // 128, 128), jnp.float32),
            jax.ShapeDtypeStruct((rows, width), jnp.float32),
            jax.ShapeDtypeStruct((rows, width), jnp.float32),
        ),
        in_specs=[vmem] * 4,
        out_specs=(hbm, hbm, hbm),
        scratch_shapes=[
            pltpu.VMEM((rows // 128, 128), jnp.float32),
            pltpu.VMEM((2, rows, width), jnp.float32),
            pltpu.SemaphoreType.DMA((2, PIECES)),
            pltpu.SemaphoreType.DMA,
        ],
        compiler_params=pltpu.CompilerParams(vmem_limit_bytes=20 * 1024 * 1024),
        cost_estimate=pl.CostEstimate(
            flops=16 * rows * width, bytes_accessed=8 * rows * width, transcendentals=2 * rows
        ),
    )(loss_acc, grads, image_emb, text_emb)
    return losses.reshape(rows), grad_image, grad_text


def solution(mesh):
    if mesh.shape["rep"] != 2 or mesh.shape["blk"] % 2:
        raise ValueError("mesh")
    return jax.shard_map(
        functools.partial(body, mesh.shape["blk"]),
        mesh=mesh,
        in_specs=(P(("blk", "rep"), None), P(("blk", "rep"), None), P(), P()),
        out_specs=(P(("blk", "rep")), P(("blk", "rep"), None), P(("blk", "rep"), None)),
        check_vma=False,
    )
```

```python
import functools

import jax
import jax.numpy as jnp
from jax import lax
from jax.experimental import pallas as pl
from jax.experimental.pallas import tpu as pltpu
from jax.sharding import PartitionSpec as P

EPSILON = 1e-06
MESH = pl.DeviceIdType.MESH
CHUNKS = 4
PIECES = 8
HALVES = 2
NT = (((1,), (1,)), ((), ()))


def row_scale(values):
    return lax.rsqrt(jnp.sum(values * values, axis=-1, keepdims=True) + EPSILON)


def kernel(
    blocks,
    log_temp,
    bias,
    image_emb,
    text_emb,
    loss_acc,
    grads,
    low,
    came,
    send_sem,
    came_sem,
):
    rows, width = image_emb.shape
    piece = rows // CHUNKS
    half = rows // HALVES
    blk, rep = lax.axis_index("blk"), lax.axis_index("rep")
    core = lax.rem(blk, 2)
    mate = (blk + 1 - 2 * core, rep)
    far = (lax.rem(blk + blocks - 1 + 2 * core, blocks), rep)
    across = (blk, 1 - rep)
    outer, inner = 1 - core, core
    straight, turned = rep == outer, rep != outer

    def chunk(c):
        return pl.ds(c * piece, piece)

    barrier = pltpu.get_barrier_semaphore()
    for other in (mate, far, across):
        pl.semaphore_signal(barrier, inc=1, device_id=other, device_id_type=MESH)

    def prepare(c):
        for side in range(2):
            emb = text_emb if side else image_emb
            values = emb[chunk(c), :].astype(jnp.float32)
            low[side, chunk(c), :] = (values * row_scale(values)).astype(jnp.bfloat16)

    def copy(kind, c, src, side, j, to):
        return pltpu.make_async_remote_copy(
            src_ref=src.at[chunk(c), :],
            dst_ref=came.at[side, j, chunk(c), :],
            send_sem=send_sem.at[kind, c],
            recv_sem=came_sem.at[side, j, c],
            device_id=to,
            device_id_type=MESH,
        )

    def far_own(c):
        return copy(0, c, low.at[1 - outer], outer, 1, far)

    def mate_own(c):
        return copy(1, c, low.at[1 - inner], inner, 1, mate)

    def far_pass(c):
        return copy(2, c, came.at[outer, 0], outer, 2, far)

    def mate_pass(c):
        return copy(3, c, came.at[inner, 0], inner, 2, mate)

    def across_own(c):
        return copy(4, c, low.at[1 - rep], rep, 0, across)

    def across_turn(c):
        return copy(5, c, came.at[1 - rep, 1], 1 - rep, 0, across)

    def got(side, j, c):
        copy(0, c, low.at[0], side, j, far).wait_recv()

    prepare(0)
    pl.semaphore_wait(barrier, 3)
    for c in range(CHUNKS):
        if c > 0:
            prepare(c)
        far_own(c).start()
        mate_own(c).start()

        @pl.when(straight)
        def _():
            across_own(c).start()

    @pl.when(turned)
    def _():
        for c in range(CHUNKS):
            got(outer, 1, c)
            across_turn(c).start()

    temper = jnp.exp(jnp.full((1, half), log_temp[0], jnp.float32))
    slope = 0.5 * temper
    shift = jnp.full((1, half), 0.5 * bias[0], jnp.float32)
    grads[...] = jnp.zeros_like(grads)
    loss_acc[...] = jnp.zeros_like(loss_acc)

    def step(side, block, h, diagonal=False):
        dots = lax.dot_general(low[side], block, NT, preferred_element_type=jnp.float32)
        turn = jnp.tanh(dots * slope + shift)
        weights = slope + slope * turn
        other_side = 1.0 - turn
        if diagonal:
            row = lax.broadcasted_iota(jnp.int32, (rows, half), 0)
            column = lax.broadcasted_iota(jnp.int32, (rows, half), 1)
            positive = row == column + h * half
            weights = jnp.where(positive, slope * turn - slope, weights)
            other_side = jnp.where(positive, 1.0 + turn, other_side)
        product = 1.0
        for at in range(0, half, 128):
            product = product * (0.5 * other_side[:, at : at + 128])
        loss_acc[side] -= jnp.log(product)
        grads[side] += jnp.dot(
            weights.astype(jnp.bfloat16), block, preferred_element_type=jnp.float32
        )

    def own_step(side):
        for h in range(HALVES):
            step(side, low[1 - side, pl.ds(h * half, half), :], h, True)

    def came_step(side, j, h):
        step(side, came[side, j, pl.ds(h * half, half), :], h)

    per = CHUNKS // HALVES

    def early(c):
        got(inner, 1, c)

        @pl.when(straight)
        def _():
            across_turn(c).start()
            got(outer, 1, c)

    def forward(c):
        got(outer, 0, c)
        far_pass(c).start()

    def late(c):
        got(inner, 0, c)
        mate_pass(c).start()

    own_step(0)
    early(0)
    own_step(1)
    early(1)
    came_step(outer, 1, 0)
    came_step(inner, 1, 0)
    early(2)
    early(3)

    @pl.when(turned)
    def _():
        for c in range(CHUNKS):
            across_own(c).start()

    forward(0)
    forward(1)
    came_step(outer, 1, 1)
    forward(2)
    came_step(inner, 1, 1)
    forward(3)
    came_step(outer, 0, 0)
    came_step(outer, 0, 1)
    late(0)
    late(1)
    came_step(inner, 0, 0)

    def last_step(side, h):
        for c in range(h * per, (h + 1) * per):
            got(side, 2, c)
        came_step(side, 2, h)

    last_step(outer, 0)
    last_step(inner, 0)
    late(2)
    late(3)
    came_step(inner, 0, 1)
    last_step(inner, 1)
    last_step(outer, 1)

    for c in range(CHUNKS):
        for sent in (far_own, mate_own, far_pass, mate_pass, across_own, across_turn):
            sent(c).wait_send()


def finish(loss_acc, grads, image_emb, text_emb, loss_out, image_out, text_out, loss, done, sem, loss_sem):
    rows = grads.shape[1]
    piece = rows // PIECES

    def store(side, c):
        part = pl.ds(c * piece, piece)
        out = text_out if side else image_out
        return pltpu.make_async_copy(done.at[side, part, :], out.at[part, :], sem.at[side, c])

    def store_loss():
        return pltpu.make_async_copy(loss, loss_out, loss_sem)

    for c in range(PIECES):
        part = pl.ds(c * piece, piece)
        for side in range(2):
            emb = text_emb if side else image_emb
            values = emb[part, :].astype(jnp.float32)
            scale = row_scale(values)
            unit = values * scale
            grad = grads[side, part, :]
            along = jnp.sum(unit * grad, axis=-1, keepdims=True)
            done[side, part, :] = scale * (grad - unit * along)
            store(side, c).start()
    for at in range(rows // 128):
        part = loss_acc[0, at * 128 : (at + 1) * 128, :]
        loss[at : at + 1, :] = jnp.sum(part.T, axis=0, keepdims=True)
    store_loss().start()
    for c in range(PIECES):
        for side in range(2):
            store(side, c).wait()
    store_loss().wait()


def body(blocks, image_emb, text_emb, log_temp, bias):
    rows, width = image_emb.shape
    vmem = pl.BlockSpec(memory_space=pltpu.VMEM)
    hbm = pl.BlockSpec(memory_space=pltpu.HBM)
    smem = pl.BlockSpec(memory_space=pltpu.SMEM)
    loss_acc, grads = pl.pallas_call(
        functools.partial(kernel, blocks),
        out_shape=(
            jax.ShapeDtypeStruct((2, rows, 128), jnp.float32),
            jax.ShapeDtypeStruct((2, rows, width), jnp.float32),
        ),
        in_specs=[smem, smem, vmem, vmem],
        out_specs=(vmem, vmem),
        scratch_shapes=[
            pltpu.VMEM((2, rows, width), jnp.bfloat16),
            pltpu.VMEM((2, 3, rows, width), jnp.bfloat16),
            pltpu.SemaphoreType.DMA((6, CHUNKS)),
            pltpu.SemaphoreType.DMA((2, 3, CHUNKS)),
        ],
        compiler_params=pltpu.CompilerParams(
            collective_id=0, has_side_effects=True, vmem_limit_bytes=44 * 1024 * 1024
        ),
        cost_estimate=pl.CostEstimate(
            flops=32 * rows * rows * width,
            bytes_accessed=12 * rows * width,
            transcendentals=14 * rows * rows,
        ),
    )(log_temp.reshape(1), bias.reshape(1), image_emb, text_emb)
    losses, grad_image, grad_text = pl.pallas_call(
        finish,
        out_shape=(
            jax.ShapeDtypeStruct((rows // 128, 128), jnp.float32),
            jax.ShapeDtypeStruct((rows, width), jnp.float32),
            jax.ShapeDtypeStruct((rows, width), jnp.float32),
        ),
        in_specs=[vmem] * 4,
        out_specs=(hbm, hbm, hbm),
        scratch_shapes=[
            pltpu.VMEM((rows // 128, 128), jnp.float32),
            pltpu.VMEM((2, rows, width), jnp.float32),
            pltpu.SemaphoreType.DMA((2, PIECES)),
            pltpu.SemaphoreType.DMA,
        ],
        compiler_params=pltpu.CompilerParams(vmem_limit_bytes=20 * 1024 * 1024),
        cost_estimate=pl.CostEstimate(
            flops=16 * rows * width, bytes_accessed=8 * rows * width, transcendentals=2 * rows
        ),
    )(loss_acc, grads, image_emb, text_emb)
    return losses.reshape(rows), grad_image, grad_text


def solution(mesh):
    if mesh.shape["rep"] != 2 or mesh.shape["blk"] % 2:
        raise ValueError("mesh")
    return jax.shard_map(
        functools.partial(body, mesh.shape["blk"]),
        mesh=mesh,
        in_specs=(P(("blk", "rep"), None), P(("blk", "rep"), None), P(), P()),
        out_specs=(P(("blk", "rep")), P(("blk", "rep"), None), P(("blk", "rep"), None)),
        check_vma=False,
    )
```
